32 devices in a mesh: rooms: 2 (over y), gx: 4 (over z), gy: 2 (over x), gz: 2 (over core).
Axes of the slice: x: 2, y: 2, z: 4, core: 2. Of those that a mesh axis runs over, the one named last changes fastest.
Arguments:
- pressure_prior: float32 [16, 64, 512], P(('rooms', 'gx'), 'gy', 'gz'), parts along dimension 0, may hold values from -6 to 6
- pressure_now: float32 [16, 64, 512], P(('rooms', 'gx'), 'gy', 'gz'), parts along dimension 0, may hold values from -6 to 6
- adjoint_end: float32 [16, 64, 512], P(('rooms', 'gx'), 'gy', 'gz'), parts along dimension 0, may hold values from -6 to 6
- adjoint_near: float32 [16, 64, 512], P(('rooms', 'gx'), 'gy', 'gz'), parts along dimension 0, may hold values from -6 to 6
- wall_faces: int32 [16, 64, 512], P(('rooms', 'gx'), 'gy', 'gz'), parts along dimension 0, may hold values from 0 to 3
- material_ids: int32 [16, 64, 512], P(('rooms', 'gx'), 'gy', 'gz'), parts along dimension 0, may hold values from 0 to 63
- admittance: float32 [64], replicated, may hold values from 0.05 to 0.6
- receivers: int32 [128, 3], P('rooms'), parts along dimension 0, may hold values from 0 to 511, as said below
- targets: float32 [128, 2], P('rooms'), parts along dimension 0, may hold values from -6 to 6
Outputs:
- adjoint_prior: float32 [16, 64, 512], P(('rooms', 'gx'), 'gy', 'gz'), parts along dimension 0
- adjoint_now: float32 [16, 64, 512], P(('rooms', 'gx'), 'gy', 'gz'), parts along dimension 0
- grad_admittance: float32 [128], P('rooms'), parts along dimension 0
The draws below stay inside these ranges and needn't reach their ends.
There are 2 independent parts, one for each index of `rooms`. The reference program is written for one: setup_inputs(seed, part) draws one part's arguments, and reference() takes and returns one part's arrays. A program takes and returns all parts, laid end to end along the dimension named above; an argument that names none is the same for every part. Nothing has to cross between parts.
Inputs may be any that keep to these rules, and one draw needn't show every extreme that they name: `receivers`: column 0 is below 8, column 1 below 64, column 2 below 512.
All inputs are finite; a program needn't handle non-finite values.
Results may differ from the reference program's by a relative error of at most 0.00015.
Values sent between devices are 32-bit elements; how exact they have to be, the bound alone decides.
A program may use at most 64 MiB of HBM per device.

```python
import math
import jax
import jax.numpy as jnp

MATERIALS = 64
RECEIVERS = 64
NX = 8
NY = 64
NZ = 512


def draw_material_ids(key, part):
    key = jax.random.fold_in(key, 11)
    first, second, third = jax.random.split(key, 3)
    shape = (NX, NY, NZ)
    strip = jnp.arange(NX, dtype=jnp.int32)[:, None, None] * (MATERIALS // 4) // NX
    strip = jnp.broadcast_to(strip, shape)
    nearby = strip * 4 + jax.random.randint(first, shape, 0, 4, dtype=jnp.int32)
    spread = jax.random.randint(second, shape, 0, MATERIALS, dtype=jnp.int32)
    picker = jax.random.randint(third, shape, 0, 10, dtype=jnp.int32)
    return jnp.where(picker == 0, spread, nearby).astype(jnp.int32)


def draw_receivers(key, part):
    key = jax.random.fold_in(key, 23)
    first, second, third = jax.random.split(key, 3)
    column_x = jax.random.randint(first, (RECEIVERS,), 0, NX, dtype=jnp.int32)
    column_y = jax.random.randint(second, (RECEIVERS,), 0, NY, dtype=jnp.int32)
    column_z = jax.random.randint(third, (RECEIVERS,), 0, NZ, dtype=jnp.int32)
    column_x = column_x.at[0].set(NX - 1).at[1].set(0)
    column_y = column_y.at[0].set(NY - 1).at[1].set(0)
    column_z = column_z.at[0].set(NZ - 1).at[1].set(0)
    return jnp.stack([column_x, column_y, column_z], axis=1).astype(jnp.int32)


def plant(array, stream_key, low, largest):
    extent = array.shape
    index_at = [jax.random.randint(jax.random.fold_in(stream_key, axis), (), 0, extent[axis]) for axis in range(len(extent))]
    array = array.at[tuple(index_at)].set(low)
    longest = extent.index(max(extent))
    index_at[longest] = (index_at[longest] + 1) % extent[longest]
    return array.at[tuple(index_at)].set(largest)


def levels(rng, extent, cuts, low, top_value):
    gain = 1.0
    for axis_at, blocks in cuts:
        draws = jax.random.uniform(jax.random.fold_in(jax.random.fold_in(rng, 6), axis_at), (blocks,), jnp.float32, low / len(cuts), top_value / len(cuts))
        gain = gain * jnp.repeat(jnp.exp(draws), extent[axis_at] // blocks).reshape((-1,) + (1,) * (len(extent) - 1 - axis_at))
    return gain


def gaussian(rng, shape, deviation, bound, cuts=(), kind=jnp.bfloat16):
    array = deviation * jax.random.normal(rng, shape, jnp.float32)
    if cuts:
        array = array * levels(rng, shape, cuts, -0.22, 0.18)
    return jnp.clip(array, -bound, bound).astype(kind)


def setup_inputs(seed: int = 0, part: int = 0) -> dict:
    keys = jax.random.split(jax.random.key(seed), 10)
    part_splits = jax.random.split(jax.random.fold_in(keys[9], part), 10)
    return {
        "pressure_prior": gaussian(part_splits[0], (NX, NY, NZ), 1.0, 6.0, ((0, 4), (1, 2), (2, 2)), jnp.float32),
        "pressure_now": gaussian(part_splits[1], (NX, NY, NZ), 1.0, 6.0, ((0, 4), (1, 2), (2, 2)), jnp.float32),
        "adjoint_end": gaussian(part_splits[2], (NX, NY, NZ), 1.0, 6.0, ((0, 4), (1, 2), (2, 2)), jnp.float32),
        "adjoint_near": gaussian(part_splits[3], (NX, NY, NZ), 1.0, 6.0, ((0, 4), (1, 2), (2, 2)), jnp.float32),
        "wall_faces": plant(jax.random.randint(part_splits[4], (NX, NY, NZ), 0, 4), jax.random.fold_in(part_splits[4], 1), 0, 3).astype(jnp.int32),
        "material_ids": draw_material_ids(jax.random.fold_in(jax.random.fold_in(keys[9], part), 71), part),
        "admittance": jnp.clip(jnp.exp(jax.random.uniform(keys[6], (MATERIALS,), jnp.float32, math.log(0.05), math.log(0.6))), 0.05, 0.6),
        "receivers": draw_receivers(jax.random.fold_in(jax.random.fold_in(keys[9], part), 71), part),
        "targets": gaussian(part_splits[8], (RECEIVERS, 2), 1.0, 6.0, (), jnp.float32),
    }


def laplace(field):
    padded = jnp.pad(field, 1)
    beside_all = padded[2:, 1:-1, 1:-1] + padded[:-2, 1:-1, 1:-1]
    beside_all = beside_all + padded[1:-1, 2:, 1:-1] + padded[1:-1, :-2, 1:-1]
    beside_all = beside_all + padded[1:-1, 1:-1, 2:] + padded[1:-1, 1:-1, :-2]
    return beside_all - 6.0 * field

def reference(pressure_prior, pressure_now, adjoint_end, adjoint_near, wall_faces, material_ids, admittance, receivers, targets):
    wall_count = wall_faces.astype(jnp.float32)

    def objective(field_prior, field_now, rate_table):
        loss_rate = 0.5 * wall_count * rate_table[material_ids]
        inverse_loss = 1.0 / (1.0 + loss_rate)
        reflect = 2.0 * inverse_loss - 1.0
        pressure_two = inverse_loss * (2.0 * field_now + 0.25 * laplace(field_now)) - reflect * field_prior
        pressure_three = inverse_loss * (2.0 * pressure_two + 0.25 * laplace(pressure_two)) - reflect * field_now
        miss_two = pressure_two[receivers[:, 0], receivers[:, 1], receivers[:, 2]] - targets[:, 0]
        miss_three = pressure_three[receivers[:, 0], receivers[:, 1], receivers[:, 2]] - targets[:, 1]
        misfit = 0.5 * jnp.sum(miss_two * miss_two) + 0.5 * jnp.sum(miss_three * miss_three)
        return misfit + jnp.sum(adjoint_end * pressure_three) + jnp.sum(adjoint_near * pressure_two)
    grad_prior, grad_now, grad_table = jax.grad(objective, argnums=(0, 1, 2))(pressure_prior, pressure_now, admittance)
    return (grad_prior, grad_now, 16.0 / math.sqrt(NX * NY * NZ) * grad_table)
```

```python
import functools
import math

import jax
import jax.numpy as jnp
from jax import lax
from jax.experimental import pallas as pl
from jax.experimental.pallas import tpu as pltpu
from jax.sharding import PartitionSpec as P

HIGHEST = lax.Precision.HIGHEST
NOW, TWO, W3, W2 = range(4)


def kernel(
    sizes,
    scaling,
    now_in,
    prior_in,
    end_in,
    near_in,
    wall_in,
    ids_in,
    table_ref,
    receivers_ref,
    targets_ref,
    prior_out,
    now_out,
    grad_out,
    now_ref,
    prior_ref,
    end_ref,
    near_ref,
    wall_ref,
    ids_ref,
    field_ref,
    result_ref,
    bins_ref,
    slots_ref,
    hx,
    hy,
    hz,
    in_sems,
    out_sems,
    send_sems,
    recv_sems,
    sum_sems,
):
    nx, ny, nz = sizes
    count = nx * ny * nz
    ix, iy, iz = lax.axis_index("gx"), lax.axis_index("gy"), lax.axis_index("gz")
    me = (ix * ny + iy) * nz + iz
    span_x, span_y, span_z = now_ref.shape
    rows = span_x * span_y
    half = span_z // 2

    def peer(step):
        other = lax.rem(me + step, count)
        return {
            "gx": other // (ny * nz),
            "gy": lax.rem(other // nz, ny),
            "gz": lax.rem(other, nz),
        }

    loads = [
        pltpu.make_async_copy(source, target, in_sems.at[i])
        for i, (source, target) in enumerate(
            (
                (ids_in, ids_ref),
                (wall_in, wall_ref),
                (now_in, now_ref),
                (prior_in, prior_ref),
                (end_in, end_ref),
                (near_in, near_ref),
            )
        )
    ]
    for load in loads:
        load.start()

    barrier = pltpu.get_barrier_semaphore()

    @pl.loop(1, count)
    def _(step):
        pl.semaphore_signal(
            barrier, inc=1, device_id=peer(step), device_id_type=pl.DeviceIdType.MESH
        )

    pl.semaphore_wait(barrier, count - 1)

    def links(level, source):
        def copy(part, target, way, where):
            return pltpu.make_async_remote_copy(
                src_ref=part,
                dst_ref=target,
                send_sem=send_sems.at[level, way],
                recv_sem=recv_sems.at[level, way],
                device_id=where,
                device_id_type=pl.DeviceIdType.MESH,
            )

        last = span_x - 1
        return (
            (copy(source.at[last], hx.at[level, 0], 0, {"gx": ix + 1}), ix < nx - 1, ix > 0),
            (copy(source.at[0], hx.at[level, 1], 1, {"gx": ix - 1}), ix > 0, ix < nx - 1),
            (
                copy(source.at[:, pl.ds(span_y - 8, 8), :], hy.at[level, 0], 2, {"gy": iy + 1}),
                iy < ny - 1,
                iy > 0,
            ),
            (
                copy(source.at[:, pl.ds(0, 8), :], hy.at[level, 1], 3, {"gy": iy - 1}),
                iy > 0,
                iy < ny - 1,
            ),
            (
                copy(
                    source.at[:, :, pl.ds(pl.multiple_of((1 - iz) * half, half), half)],
                    hz.at[level],
                    4,
                    {"gz": 1 - iz},
                ),
                None,
                None,
            ),
        )

    def when(test, act):
        if test is None:
            act()
        else:
            pl.when(test)(act)

    def send(level, source):
        for copy, sends, _ in links(level, source):
            when(sends, copy.start)

    def receive(level, source):
        for copy, _, receives in links(level, source):
            when(receives, copy.wait_recv)

    def sent(level, source):
        for copy, sends, _ in links(level, source):
            when(sends, copy.wait_send)

    send(NOW, now_in)

    for test, buffer, side in (
        (ix == 0, hx, 0),
        (ix == nx - 1, hx, 1),
        (iy == 0, hy, 0),
        (iy == ny - 1, hy, 1),
    ):

        @pl.when(test)
        def _():
            for level in range(4):
                buffer[level, side] = jnp.zeros(buffer.shape[2:], jnp.float32)

    row = lax.broadcasted_iota(jnp.int32, (rows, span_z), 0)
    lane = lax.broadcasted_iota(jnp.int32, (rows, span_z), 1)
    top = lax.rem(row, span_y) == 0
    bottom = lax.rem(row, span_y) == span_y - 1

    def laplace(field, level):
        before_x = jnp.concatenate([hx[level, 0], field[: rows - span_y]], axis=0)
        after_x = jnp.concatenate([field[span_y:], hx[level, 1]], axis=0)
        shape = (span_x, span_y, span_z)
        before_y = jnp.broadcast_to(hy[level, 0][:, 7:8, :], shape).reshape(rows, span_z)
        after_y = jnp.broadcast_to(hy[level, 1][:, 0:1, :], shape).reshape(rows, span_z)
        before_y = jnp.where(top, before_y, pltpu.roll(field, 1, 0))
        after_y = jnp.where(bottom, after_y, pltpu.roll(field, rows - 1, 0))
        beside = hz[level].reshape(rows, half)
        before_z = jnp.where(iz == 1, beside[:, half - 1 :], 0.0)
        after_z = jnp.where(iz == 0, beside[:, :1], 0.0)
        before_z = jnp.where(lane == 0, before_z, pltpu.roll(field, 1, 1))
        after_z = jnp.where(lane == span_z - 1, after_z, pltpu.roll(field, span_z - 1, 1))
        total = before_x + after_x + before_y + after_y + before_z + after_z
        return total - 6.0 * field

    def flat(ref):
        return ref[...].reshape(rows, span_z)

    place = receivers_ref[...]
    at_x = place[:, 0:1] - ix * span_x
    at_y = place[:, 1:2] - iy * span_y
    at_z = place[:, 2:3] - iz * span_z
    inside = (at_x >= 0) & (at_x < span_x) & (at_y >= 0) & (at_y < span_y)
    inside = inside & (at_z >= 0) & (at_z < span_z)
    spots = place.shape[0]
    at_row = jnp.where(inside, at_x * span_y + at_y, -1)
    in_row = lax.broadcasted_iota(jnp.int32, (spots, rows), 1) == at_row
    in_row = in_row.astype(jnp.float32)
    in_lane = lax.broadcasted_iota(jnp.int32, (spots, span_z), 1) == at_z
    in_lane = in_lane.astype(jnp.float32)

    def misfit(field, column):
        lines = lax.dot_general(
            in_row, field, (((1,), (0,)), ((), ())), precision=HIGHEST,
            preferred_element_type=jnp.float32,
        )
        values = jnp.sum(lines * in_lane, axis=1, keepdims=True)
        mismatch = jnp.where(inside, values - targets_ref[:, column : column + 1], 0.0)
        return lax.dot_general(
            in_row, in_lane * mismatch, (((0,), (0,)), ((), ())), precision=HIGHEST,
            preferred_element_type=jnp.float32,
        )

    for load in loads[:2]:
        load.wait()
    ids = flat(ids_ref)
    walls = 0.5 * flat(wall_ref).astype(jnp.float32)
    table = jnp.broadcast_to(table_ref[...], (rows, 128))
    rate = jnp.concatenate(
        [
            jnp.take_along_axis(table, ids[:, i : i + 128], axis=1, mode="promise_in_bounds")
            for i in range(0, span_z, 128)
        ],
        axis=1,
    )
    inverse_loss = 1.0 / (1.0 + walls * rate)
    reflect = 2.0 * inverse_loss - 1.0

    for load in loads[2:]:
        load.wait()
    now = flat(now_ref)
    prior = flat(prior_ref)
    receive(NOW, now_in)
    two = inverse_loss * (2.0 * now + 0.25 * laplace(now, NOW)) - reflect * prior
    field_ref[TWO] = two.reshape(now_ref.shape)
    send(TWO, field_ref.at[TWO])
    incoming = flat(near_ref) + misfit(two, 0)

    receive(TWO, field_ref.at[TWO])
    three = inverse_loss * (2.0 * two + 0.25 * laplace(two, TWO)) - reflect * now
    adjoint_three = flat(end_ref) + misfit(three, 1)
    weighted_three = inverse_loss * adjoint_three
    field_ref[W3] = weighted_three.reshape(now_ref.shape)
    send(W3, field_ref.at[W3])
    term_three = weighted_three * (now - three)

    receive(W3, field_ref.at[W3])
    adjoint_two = incoming + 2.0 * weighted_three + 0.25 * laplace(weighted_three, W3)
    weighted_two = inverse_loss * adjoint_two
    field_ref[W2] = weighted_two.reshape(now_ref.shape)
    send(W2, field_ref.at[W2])

    terms = walls * (term_three + weighted_two * (prior - two))
    kinds = bins_ref.shape[0]

    @pl.loop(0, kinds, unroll=8)
    def _(kind):
        mine = jnp.where(ids == kind, terms, 0.0)
        mine = jnp.sum(mine.reshape(rows // 8, 8, span_z), axis=0)
        bins_ref[kind] = mine[:, :128] + mine[:, 128:]

    bins = jnp.sum(bins_ref[...], axis=1)
    ones = jnp.ones((8, 128), jnp.float32)
    sums = lax.dot_general(
        ones, bins, (((1,), (1,)), ((), ())), precision=HIGHEST,
        preferred_element_type=jnp.float32,
    )
    slots_ref[me] = jnp.concatenate([sums[:1], sums[:1]], axis=1)

    @pl.loop(1, count)
    def _(step):
        pltpu.make_async_remote_copy(
            src_ref=slots_ref.at[me],
            dst_ref=slots_ref.at[me],
            send_sem=sum_sems.at[0],
            recv_sem=sum_sems.at[1],
            device_id=peer(step),
            device_id_type=pl.DeviceIdType.MESH,
        ).start()

    result_ref[0] = (-reflect * adjoint_two).reshape(now_ref.shape)
    prior_copy = pltpu.make_async_copy(result_ref.at[0], prior_out, out_sems.at[0])
    prior_copy.start()

    receive(W2, field_ref.at[W2])
    result = -reflect * adjoint_three + 2.0 * weighted_two + 0.25 * laplace(weighted_two, W2)
    result_ref[1] = result.reshape(now_ref.shape)
    now_copy = pltpu.make_async_copy(result_ref.at[1], now_out, out_sems.at[1])
    now_copy.start()

    others = pltpu.make_async_remote_copy(
        src_ref=slots_ref.at[pl.ds(0, count - 1)],
        dst_ref=slots_ref.at[pl.ds(0, count - 1)],
        send_sem=sum_sems.at[0],
        recv_sem=sum_sems.at[1],
        device_id=peer(1),
        device_id_type=pl.DeviceIdType.MESH,
    )
    others.wait_recv()
    grad_out[...] = scaling * jnp.sum(slots_ref[...], axis=0)
    others.wait_send()
    sent(NOW, now_in)
    for level in (TWO, W3, W2):
        sent(level, field_ref.at[level])
    prior_copy.wait()
    now_copy.wait()


def local(
    sizes,
    pressure_prior,
    pressure_now,
    adjoint_end,
    adjoint_near,
    wall_faces,
    material_ids,
    admittance,
    receivers,
    targets,
):
    shape = pressure_now.shape
    span_x, span_y, span_z = shape
    count = math.prod(sizes)
    kinds = admittance.shape[0]
    scaling = 16.0 / math.sqrt(pressure_now.size * count)
    table = jnp.concatenate([admittance, admittance]).reshape(1, 2 * kinds)
    anywhere = pl.BlockSpec(memory_space=pl.ANY)
    in_vmem = pl.BlockSpec(memory_space=pltpu.VMEM)
    block = pltpu.VMEM(shape, jnp.float32)
    prior_out, now_out, grad = pl.pallas_call(
        functools.partial(kernel, sizes, scaling),
        out_shape=(
            jax.ShapeDtypeStruct(shape, jnp.float32),
            jax.ShapeDtypeStruct(shape, jnp.float32),
            jax.ShapeDtypeStruct((1, 128), jnp.float32),
        ),
        in_specs=[anywhere] * 6 + [in_vmem] * 3,
        out_specs=(anywhere, anywhere, in_vmem),
        scratch_shapes=[
            block,
            block,
            block,
            block,
            pltpu.VMEM(shape, jnp.int32),
            pltpu.VMEM(shape, jnp.int32),
            pltpu.VMEM((4,) + shape, jnp.float32),
            pltpu.VMEM((2,) + shape, jnp.float32),
            pltpu.VMEM((kinds, 8, 128), jnp.float32),
            pltpu.VMEM((count, 1, 128), jnp.float32),
            pltpu.VMEM((4, 2, span_y, span_z), jnp.float32),
            pltpu.VMEM((4, 2, span_x, 8, span_z), jnp.float32),
            pltpu.VMEM((4, span_x, span_y, span_z // 2), jnp.float32),
            pltpu.SemaphoreType.DMA((6,)),
            pltpu.SemaphoreType.DMA((2,)),
            pltpu.SemaphoreType.DMA((4, 5)),
            pltpu.SemaphoreType.DMA((4, 5)),
            pltpu.SemaphoreType.DMA((2,)),
        ],
        compiler_params=pltpu.CompilerParams(
            collective_id=0, has_side_effects=True, vmem_limit_bytes=32 * 1024 * 1024
        ),
    )(
        pressure_now,
        pressure_prior,
        adjoint_end,
        adjoint_near,
        wall_faces,
        material_ids,
        table,
        receivers,
        targets,
    )
    return prior_out, now_out, grad[0, :kinds]


def solution(mesh):
    cells = P(("rooms", "gx"), "gy", "gz")
    sizes = tuple(mesh.shape[axis] for axis in ("gx", "gy", "gz"))
    return jax.shard_map(
        functools.partial(local, sizes),
        mesh=mesh,
        in_specs=(cells,) * 6 + (P(), P("rooms", None), P("rooms", None)),
        out_specs=(cells, cells, P("rooms")),
        check_vma=False,
    )
```

```python
import functools
import math

import jax
import jax.numpy as jnp
from jax import lax
from jax.experimental import pallas as pl
from jax.experimental.pallas import tpu as pltpu
from jax.sharding import PartitionSpec as P

VMEM_BYTES = 64 * 1024 * 1024
HIGHEST = lax.Precision.HIGHEST
NOW, TWO, W3, W2 = range(4)


def kernel(
    sizes,
    scaling,
    now_in,
    prior_in,
    end_in,
    near_in,
    wall_in,
    ids_in,
    table_ref,
    receivers_ref,
    targets_ref,
    prior_out,
    now_out,
    grad_out,
    now_ref,
    prior_ref,
    end_ref,
    near_ref,
    wall_ref,
    ids_ref,
    field_ref,
    result_ref,
    bins_ref,
    slots_ref,
    hx,
    hy,
    hz,
    in_sems,
    out_sems,
    send_sems,
    recv_sems,
    sum_sems,
):
    nx, ny, nz = sizes
    count = nx * ny * nz
    ix, iy, iz = lax.axis_index("gx"), lax.axis_index("gy"), lax.axis_index("gz")
    me = (ix * ny + iy) * nz + iz
    span_x, span_y, span_z = now_ref.shape
    rows = span_x * span_y
    half = span_z // 2

    def peer(step):
        other = lax.rem(me + step, count)
        return {
            "gx": other // (ny * nz),
            "gy": lax.rem(other // nz, ny),
            "gz": lax.rem(other, nz),
        }

    loads = [
        pltpu.make_async_copy(source, target, in_sems.at[i])
        for i, (source, target) in enumerate(
            (
                (ids_in, ids_ref),
                (wall_in, wall_ref),
                (now_in, now_ref),
                (prior_in, prior_ref),
                (end_in, end_ref),
                (near_in, near_ref),
            )
        )
    ]
    for load in loads:
        load.start()

    barrier = pltpu.get_barrier_semaphore()

    @pl.loop(1, count)
    def _(step):
        pl.semaphore_signal(
            barrier, inc=1, device_id=peer(step), device_id_type=pl.DeviceIdType.MESH
        )

    pl.semaphore_wait(barrier, count - 1)

    def links(level, source):
        def copy(part, target, way, where):
            return pltpu.make_async_remote_copy(
                src_ref=part,
                dst_ref=target,
                send_sem=send_sems.at[level, way],
                recv_sem=recv_sems.at[level, way],
                device_id=where,
                device_id_type=pl.DeviceIdType.MESH,
            )

        last = span_x - 1
        return (
            (copy(source.at[last], hx.at[level, 0], 0, {"gx": ix + 1}), ix < nx - 1, ix > 0),
            (copy(source.at[0], hx.at[level, 1], 1, {"gx": ix - 1}), ix > 0, ix < nx - 1),
            (
                copy(source.at[:, pl.ds(span_y - 8, 8), :], hy.at[level, 0], 2, {"gy": iy + 1}),
                iy < ny - 1,
                iy > 0,
            ),
            (
                copy(source.at[:, pl.ds(0, 8), :], hy.at[level, 1], 3, {"gy": iy - 1}),
                iy > 0,
                iy < ny - 1,
            ),
            (
                copy(
                    source.at[:, :, pl.ds(pl.multiple_of((1 - iz) * half, half), half)],
                    hz.at[level],
                    4,
                    {"gz": 1 - iz},
                ),
                None,
                None,
            ),
        )

    def when(test, act):
        if test is None:
            act()
        else:
            pl.when(test)(act)

    def send(level, source):
        for copy, sends, _ in links(level, source):
            when(sends, copy.start)

    def receive(level, source):
        for copy, _, receives in links(level, source):
            when(receives, copy.wait_recv)

    def sent(level, source):
        for copy, sends, _ in links(level, source):
            when(sends, copy.wait_send)

    send(NOW, now_in)

    for test, buffer, side in (
        (ix == 0, hx, 0),
        (ix == nx - 1, hx, 1),
        (iy == 0, hy, 0),
        (iy == ny - 1, hy, 1),
    ):

        @pl.when(test)
        def _():
            for level in range(4):
                buffer[level, side] = jnp.zeros(buffer.shape[2:], jnp.float32)

    row = lax.broadcasted_iota(jnp.int32, (rows, span_z), 0)
    lane = lax.broadcasted_iota(jnp.int32, (rows, span_z), 1)
    top = lax.rem(row, span_y) == 0
    bottom = lax.rem(row, span_y) == span_y - 1

    def laplace(field, level):
        before_x = jnp.concatenate([hx[level, 0], field[: rows - span_y]], axis=0)
        after_x = jnp.concatenate([field[span_y:], hx[level, 1]], axis=0)
        shape = (span_x, span_y, span_z)
        before_y = jnp.broadcast_to(hy[level, 0][:, 7:8, :], shape).reshape(rows, span_z)
        after_y = jnp.broadcast_to(hy[level, 1][:, 0:1, :], shape).reshape(rows, span_z)
        before_y = jnp.where(top, before_y, pltpu.roll(field, 1, 0))
        after_y = jnp.where(bottom, after_y, pltpu.roll(field, rows - 1, 0))
        beside = hz[level].reshape(rows, half)
        before_z = jnp.where(iz == 1, beside[:, half - 1 :], 0.0)
        after_z = jnp.where(iz == 0, beside[:, :1], 0.0)
        before_z = jnp.where(lane == 0, before_z, pltpu.roll(field, 1, 1))
        after_z = jnp.where(lane == span_z - 1, after_z, pltpu.roll(field, span_z - 1, 1))
        total = before_x + after_x + before_y + after_y + before_z + after_z
        return total - 6.0 * field

    def flat(ref):
        return ref[...].reshape(rows, span_z)

    place = receivers_ref[...]
    spots = place.shape[1]
    at_x = place[0:1] - ix * span_x
    at_y = place[1:2] - iy * span_y
    at_z = place[2:3] - iz * span_z
    inside = (at_x >= 0) & (at_x < span_x) & (at_y >= 0) & (at_y < span_y)
    inside = inside & (at_z >= 0) & (at_z < span_z)
    at_row = jnp.where(inside, at_x * span_y + at_y, -1)
    in_row = lax.broadcasted_iota(jnp.int32, (rows, spots), 0) == at_row
    in_row = in_row.astype(jnp.float32)
    in_lane = lax.broadcasted_iota(jnp.int32, (span_z, spots), 0) == at_z
    in_lane = in_lane.astype(jnp.float32).astype(jnp.bfloat16)

    def exact(values, pattern, dims):
        parts = []
        rest = values
        for _ in range(3):
            part = rest.astype(jnp.bfloat16)
            rest = rest - part.astype(jnp.float32)
            parts.append(part)
        product = lax.dot_general(
            jnp.concatenate(parts, axis=0), pattern, (dims, ((), ())),
            preferred_element_type=jnp.float32,
        )
        high, middle, low = jnp.split(product, 3, axis=0)
        return high + (middle + low)

    def misfit(field, column):
        lines = exact(field, in_lane, ((1,), (0,)))
        values = jnp.sum(lines * in_row, axis=0, keepdims=True)
        mismatch = jnp.where(inside, values - targets_ref[column : column + 1], 0.0)
        return exact(in_row * mismatch, in_lane, ((1,), (1,)))

    for load in loads[:2]:
        load.wait()
    ids = flat(ids_ref)
    walls = 0.5 * flat(wall_ref).astype(jnp.float32)
    table = table_ref[...]
    table = jnp.broadcast_to(jnp.concatenate([table, table], axis=1), (rows, 128))
    rate = jnp.concatenate(
        [
            jnp.take_along_axis(table, ids[:, i : i + 128], axis=1, mode="promise_in_bounds")
            for i in range(0, span_z, 128)
        ],
        axis=1,
    )
    inverse_loss = 1.0 / (1.0 + walls * rate)
    reflect = 2.0 * inverse_loss - 1.0

    for load in loads[2:]:
        load.wait()
    now = flat(now_ref)
    prior = flat(prior_ref)
    receive(NOW, now_in)
    two = inverse_loss * (2.0 * now + 0.25 * laplace(now, NOW)) - reflect * prior
    field_ref[TWO] = two.reshape(now_ref.shape)
    send(TWO, field_ref.at[TWO])
    incoming = flat(near_ref) + misfit(two, 0)

    receive(TWO, field_ref.at[TWO])
    three = inverse_loss * (2.0 * two + 0.25 * laplace(two, TWO)) - reflect * now
    adjoint_three = flat(end_ref) + misfit(three, 1)
    weighted_three = inverse_loss * adjoint_three
    field_ref[W3] = weighted_three.reshape(now_ref.shape)
    send(W3, field_ref.at[W3])
    term_three = weighted_three * (now - three)

    receive(W3, field_ref.at[W3])
    adjoint_two = incoming + 2.0 * weighted_three + 0.25 * laplace(weighted_three, W3)
    weighted_two = inverse_loss * adjoint_two
    field_ref[W2] = weighted_two.reshape(now_ref.shape)
    send(W2, field_ref.at[W2])

    terms = walls * (term_three + weighted_two * (prior - two))
    kinds = bins_ref.shape[0]

    @pl.loop(0, kinds, unroll=8)
    def _(kind):
        mine = jnp.where(ids == kind, terms, 0.0)
        mine = jnp.sum(mine.reshape(rows // 8, 8, span_z), axis=0)
        bins_ref[kind] = mine[:, :128] + mine[:, 128:]

    bins = jnp.sum(bins_ref[...], axis=1)
    ones = jnp.ones((8, 128), jnp.float32)
    sums = lax.dot_general(
        ones, bins, (((1,), (1,)), ((), ())), precision=HIGHEST,
        preferred_element_type=jnp.float32,
    )
    slots_ref[me] = jnp.concatenate([sums[:1], sums[:1]], axis=1)

    @pl.loop(1, count)
    def _(step):
        pltpu.make_async_remote_copy(
            src_ref=slots_ref.at[me],
            dst_ref=slots_ref.at[me],
            send_sem=sum_sems.at[0],
            recv_sem=sum_sems.at[1],
            device_id=peer(step),
            device_id_type=pl.DeviceIdType.MESH,
        ).start()

    result_ref[0] = (-reflect * adjoint_two).reshape(now_ref.shape)
    prior_copy = pltpu.make_async_copy(result_ref.at[0], prior_out, out_sems.at[0])
    prior_copy.start()

    receive(W2, field_ref.at[W2])
    result = -reflect * adjoint_three + 2.0 * weighted_two + 0.25 * laplace(weighted_two, W2)
    result_ref[1] = result.reshape(now_ref.shape)
    now_copy = pltpu.make_async_copy(result_ref.at[1], now_out, out_sems.at[1])
    now_copy.start()

    others = pltpu.make_async_remote_copy(
        src_ref=slots_ref.at[pl.ds(0, count - 1)],
        dst_ref=slots_ref.at[pl.ds(0, count - 1)],
        send_sem=sum_sems.at[0],
        recv_sem=sum_sems.at[1],
        device_id=peer(1),
        device_id_type=pl.DeviceIdType.MESH,
    )
    others.wait_recv()
    grad_out[...] = scaling * jnp.sum(slots_ref[...], axis=0)[:, : grad_out.shape[1]]
    others.wait_send()
    sent(NOW, now_in)
    for level in (TWO, W3, W2):
        sent(level, field_ref.at[level])
    prior_copy.wait()
    now_copy.wait()


def write(prior_in, now_in, grad_in, prior_out, now_out, grad_out, sems):
    copies = [
        pltpu.make_async_copy(prior_in, prior_out, sems.at[0]),
        pltpu.make_async_copy(now_in, now_out, sems.at[1]),
        pltpu.make_async_copy(grad_in, grad_out, sems.at[2]),
    ]
    for copy in copies:
        copy.start()
    for copy in copies:
        copy.wait()


def local(
    sizes,
    pressure_prior,
    pressure_now,
    adjoint_end,
    adjoint_near,
    wall_faces,
    material_ids,
    admittance,
    receivers,
    targets,
):
    shape = pressure_now.shape
    span_x, span_y, span_z = shape
    count = math.prod(sizes)
    kinds = admittance.shape[0]
    scaling = 16.0 / math.sqrt(pressure_now.size * count)
    in_hbm = pl.BlockSpec(memory_space=pltpu.HBM)
    in_vmem = pl.BlockSpec(memory_space=pltpu.VMEM)
    block = pltpu.VMEM(shape, jnp.float32)
    prior_out, now_out, grad = pl.pallas_call(
        functools.partial(kernel, sizes, scaling),
        out_shape=(
            jax.ShapeDtypeStruct(shape, jnp.float32),
            jax.ShapeDtypeStruct(shape, jnp.float32),
            jax.ShapeDtypeStruct((1, kinds), jnp.float32),
        ),
        in_specs=[in_hbm] * 6 + [in_vmem] * 3,
        out_specs=(in_hbm, in_hbm, in_vmem),
        scratch_shapes=[
            block,
            block,
            block,
            block,
            pltpu.VMEM(shape, jnp.int32),
            pltpu.VMEM(shape, jnp.int32),
            pltpu.VMEM((4,) + shape, jnp.float32),
            pltpu.VMEM((2,) + shape, jnp.float32),
            pltpu.VMEM((kinds, 8, 128), jnp.float32),
            pltpu.VMEM((count, 1, 128), jnp.float32),
            pltpu.VMEM((4, 2, span_y, span_z), jnp.float32),
            pltpu.VMEM((4, 2, span_x, 8, span_z), jnp.float32),
            pltpu.VMEM((4, span_x, span_y, span_z // 2), jnp.float32),
            pltpu.SemaphoreType.DMA((6,)),
            pltpu.SemaphoreType.DMA((2,)),
            pltpu.SemaphoreType.DMA((4, 5)),
            pltpu.SemaphoreType.DMA((4, 5)),
            pltpu.SemaphoreType.DMA((2,)),
        ],
        compiler_params=pltpu.CompilerParams(
            collective_id=0, has_side_effects=True, vmem_limit_bytes=VMEM_BYTES
        ),
    )(
        pressure_now,
        pressure_prior,
        adjoint_end,
        adjoint_near,
        wall_faces,
        material_ids,
        admittance.reshape(1, kinds),
        receivers.T,
        targets.T,
    )
    results = (prior_out, now_out, grad)
    prior_out, now_out, grad = pl.pallas_call(
        write,
        out_shape=(
            jax.ShapeDtypeStruct(shape, jnp.float32),
            jax.ShapeDtypeStruct(shape, jnp.float32),
            jax.ShapeDtypeStruct((1, kinds), jnp.float32),
        ),
        in_specs=[in_hbm] * 3,
        out_specs=(in_hbm,) * 3,
        scratch_shapes=[pltpu.SemaphoreType.DMA((3,))],
        compiler_params=pltpu.CompilerParams(vmem_limit_bytes=VMEM_BYTES),
    )(*results)
    return prior_out, now_out, grad.reshape(kinds)


def solution(mesh):
    cells = P(("rooms", "gx"), "gy", "gz")
    sizes = tuple(mesh.shape[axis] for axis in ("gx", "gy", "gz"))
    return jax.shard_map(
        functools.partial(local, sizes),
        mesh=mesh,
        in_specs=(cells,) * 6 + (P(), P("rooms", None), P("rooms", None)),
        out_specs=(cells, cells, P("rooms")),
        check_vma=False,
    )
```

```python
import functools
import math

import jax
import jax.numpy as jnp
from jax import lax
from jax.experimental import pallas as pl
from jax.experimental.pallas import tpu as pltpu
from jax.sharding import PartitionSpec as P

VMEM_BYTES = 64 * 1024 * 1024
HIGHEST = lax.Precision.HIGHEST
NOW, TWO, W3, W2 = range(4)


def kernel(
    sizes,
    scaling,
    now_in,
    prior_in,
    end_in,
    near_in,
    wall_in,
    ids_in,
    table_ref,
    receivers_ref,
    targets_ref,
    prior_out,
    now_out,
    grad_out,
    now_ref,
    prior_ref,
    end_ref,
    near_ref,
    wall_ref,
    ids_ref,
    field_ref,
    result_ref,
    bins_ref,
    slots_ref,
    hx,
    hy,
    hz,
    in_sems,
    out_sems,
    send_sems,
    recv_sems,
    sum_sems,
):
    nx, ny, nz = sizes
    count = nx * ny * nz
    ix, iy, iz = lax.axis_index("gx"), lax.axis_index("gy"), lax.axis_index("gz")
    me = (ix * ny + iy) * nz + iz
    span_x, span_y, span_z = now_ref.shape
    rows = span_x * span_y
    half = span_z // 2

    def peer(step):
        other = lax.rem(me + step, count)
        return {
            "gx": other // (ny * nz),
            "gy": lax.rem(other // nz, ny),
            "gz": lax.rem(other, nz),
        }

    loads = [
        pltpu.make_async_copy(source, target, in_sems.at[i])
        for i, (source, target) in enumerate(
            (
                (ids_in, ids_ref),
                (wall_in, wall_ref),
                (now_in, now_ref),
                (prior_in, prior_ref),
                (end_in, end_ref),
                (near_in, near_ref),
            )
        )
    ]
    for load in loads:
        load.start()

    barrier = pltpu.get_barrier_semaphore()

    @pl.loop(1, count)
    def _(step):
        pl.semaphore_signal(
            barrier, inc=1, device_id=peer(step), device_id_type=pl.DeviceIdType.MESH
        )

    pl.semaphore_wait(barrier, count - 1)

    def links(level, source):
        def copy(part, target, way, where):
            return pltpu.make_async_remote_copy(
                src_ref=part,
                dst_ref=target,
                send_sem=send_sems.at[level, way],
                recv_sem=recv_sems.at[level, way],
                device_id=where,
                device_id_type=pl.DeviceIdType.MESH,
            )

        last = span_x - 1
        return (
            (copy(source.at[last], hx.at[level, 0], 0, {"gx": ix + 1}), ix < nx - 1, ix > 0),
            (copy(source.at[0], hx.at[level, 1], 1, {"gx": ix - 1}), ix > 0, ix < nx - 1),
            (
                copy(source.at[:, pl.ds(span_y - 8, 8), :], hy.at[level, 0], 2, {"gy": iy + 1}),
                iy < ny - 1,
                iy > 0,
            ),
            (
                copy(source.at[:, pl.ds(0, 8), :], hy.at[level, 1], 3, {"gy": iy - 1}),
                iy > 0,
                iy < ny - 1,
            ),
            (
                copy(
                    source.at[:, :, pl.ds(pl.multiple_of((1 - iz) * half, half), half)],
                    hz.at[level],
                    4,
                    {"gz": 1 - iz},
                ),
                None,
                None,
            ),
        )

    def when(test, act):
        if test is None:
            act()
        else:
            pl.when(test)(act)

    def send(level, source):
        for copy, sends, _ in links(level, source):
            when(sends, copy.start)

    def receive(level, source):
        for copy, _, receives in links(level, source):
            when(receives, copy.wait_recv)

    def sent(level, source):
        for copy, sends, _ in links(level, source):
            when(sends, copy.wait_send)

    send(NOW, now_in)

    for test, buffer, side in (
        (ix == 0, hx, 0),
        (ix == nx - 1, hx, 1),
        (iy == 0, hy, 0),
        (iy == ny - 1, hy, 1),
    ):

        @pl.when(test)
        def _():
            for level in range(4):
                buffer[level, side] = jnp.zeros(buffer.shape[2:], jnp.float32)

    row = lax.broadcasted_iota(jnp.int32, (rows, span_z), 0)
    lane = lax.broadcasted_iota(jnp.int32, (rows, span_z), 1)
    top = lax.rem(row, span_y) == 0
    bottom = lax.rem(row, span_y) == span_y - 1

    def laplace(field, level):
        before_x = jnp.concatenate([hx[level, 0], field[: rows - span_y]], axis=0)
        after_x = jnp.concatenate([field[span_y:], hx[level, 1]], axis=0)
        shape = (span_x, span_y, span_z)
        before_y = jnp.broadcast_to(hy[level, 0][:, 7:8, :], shape).reshape(rows, span_z)
        after_y = jnp.broadcast_to(hy[level, 1][:, 0:1, :], shape).reshape(rows, span_z)
        before_y = jnp.where(top, before_y, pltpu.roll(field, 1, 0))
        after_y = jnp.where(bottom, after_y, pltpu.roll(field, rows - 1, 0))
        beside = hz[level].reshape(rows, half)
        before_z = jnp.where(iz == 1, beside[:, half - 1 :], 0.0)
        after_z = jnp.where(iz == 0, beside[:, :1], 0.0)
        before_z = jnp.where(lane == 0, before_z, pltpu.roll(field, 1, 1))
        after_z = jnp.where(lane == span_z - 1, after_z, pltpu.roll(field, span_z - 1, 1))
        total = before_x + after_x + before_y + after_y + before_z + after_z
        return total - 6.0 * field

    def flat(ref):
        return ref[...].reshape(rows, span_z)

    place = receivers_ref[...]
    spots = place.shape[1]
    at_x = place[0:1] - ix * span_x
    at_y = place[1:2] - iy * span_y
    at_z = place[2:3] - iz * span_z
    inside = (at_x >= 0) & (at_x < span_x) & (at_y >= 0) & (at_y < span_y)
    inside = inside & (at_z >= 0) & (at_z < span_z)
    at_row = jnp.where(inside, at_x * span_y + at_y, -1)
    in_row = lax.broadcasted_iota(jnp.int32, (rows, spots), 0) == at_row
    in_row = in_row.astype(jnp.float32)
    in_lane = lax.broadcasted_iota(jnp.int32, (span_z, spots), 0) == at_z
    in_lane = in_lane.astype(jnp.float32).astype(jnp.bfloat16)

    def exact(values, pattern, dims):
        parts = []
        rest = values
        for _ in range(3):
            part = rest.astype(jnp.bfloat16)
            rest = rest - part.astype(jnp.float32)
            parts.append(part)
        product = lax.dot_general(
            jnp.concatenate(parts, axis=0), pattern, (dims, ((), ())),
            preferred_element_type=jnp.float32,
        )
        high, middle, low = jnp.split(product, 3, axis=0)
        return high + (middle + low)

    def misfit(field, column):
        lines = exact(field, in_lane, ((1,), (0,)))
        values = jnp.sum(lines * in_row, axis=0, keepdims=True)
        mismatch = jnp.where(inside, values - targets_ref[column : column + 1], 0.0)
        return exact(in_row * mismatch, in_lane, ((1,), (1,)))

    for load in loads[:2]:
        load.wait()
    ids = flat(ids_ref)
    walls = 0.5 * flat(wall_ref).astype(jnp.float32)
    table = table_ref[...]
    table = jnp.broadcast_to(jnp.concatenate([table, table], axis=1), (rows, 128))
    rate = jnp.concatenate(
        [
            jnp.take_along_axis(table, ids[:, i : i + 128], axis=1, mode="promise_in_bounds")
            for i in range(0, span_z, 128)
        ],
        axis=1,
    )
    inverse_loss = 1.0 / (1.0 + walls * rate)
    reflect = 2.0 * inverse_loss - 1.0

    for load in loads[2:]:
        load.wait()
    now = flat(now_ref)
    prior = flat(prior_ref)
    receive(NOW, now_in)
    two = inverse_loss * (2.0 * now + 0.25 * laplace(now, NOW)) - reflect * prior
    field_ref[TWO] = two.reshape(now_ref.shape)
    send(TWO, field_ref.at[TWO])
    incoming = flat(near_ref) + misfit(two, 0)

    receive(TWO, field_ref.at[TWO])
    three = inverse_loss * (2.0 * two + 0.25 * laplace(two, TWO)) - reflect * now
    adjoint_three = flat(end_ref) + misfit(three, 1)
    weighted_three = inverse_loss * adjoint_three
    field_ref[W3] = weighted_three.reshape(now_ref.shape)
    send(W3, field_ref.at[W3])
    term_three = weighted_three * (now - three)

    receive(W3, field_ref.at[W3])
    adjoint_two = incoming + 2.0 * weighted_three + 0.25 * laplace(weighted_three, W3)
    weighted_two = inverse_loss * adjoint_two
    field_ref[W2] = weighted_two.reshape(now_ref.shape)
    send(W2, field_ref.at[W2])

    terms = walls * (term_three + weighted_two * (prior - two))
    kinds = bins_ref.shape[0]

    @pl.loop(0, kinds, unroll=8)
    def _(kind):
        mine = jnp.where(ids == kind, terms, 0.0)
        mine = jnp.sum(mine.reshape(rows // 8, 8, span_z), axis=0)
        bins_ref[kind] = mine[:, :128] + mine[:, 128:]

    bins = jnp.sum(bins_ref[...], axis=1)
    ones = jnp.ones((8, 128), jnp.float32)
    sums = lax.dot_general(
        ones, bins, (((1,), (1,)), ((), ())), precision=HIGHEST,
        preferred_element_type=jnp.float32,
    )
    slots_ref[me] = jnp.concatenate([sums[:1], sums[:1]], axis=1)

    @pl.loop(1, count)
    def _(step):
        pltpu.make_async_remote_copy(
            src_ref=slots_ref.at[me],
            dst_ref=slots_ref.at[me],
            send_sem=sum_sems.at[0],
            recv_sem=sum_sems.at[1],
            device_id=peer(step),
            device_id_type=pl.DeviceIdType.MESH,
        ).start()

    result_ref[0] = (-reflect * adjoint_two).reshape(now_ref.shape)
    prior_copy = pltpu.make_async_copy(result_ref.at[0], prior_out, out_sems.at[0])
    prior_copy.start()

    receive(W2, field_ref.at[W2])
    result = -reflect * adjoint_three + 2.0 * weighted_two + 0.25 * laplace(weighted_two, W2)
    result_ref[1] = result.reshape(now_ref.shape)
    now_copy = pltpu.make_async_copy(result_ref.at[1], now_out, out_sems.at[1])
    now_copy.start()

    others = pltpu.make_async_remote_copy(
        src_ref=slots_ref.at[pl.ds(0, count - 1)],
        dst_ref=slots_ref.at[pl.ds(0, count - 1)],
        send_sem=sum_sems.at[0],
        recv_sem=sum_sems.at[1],
        device_id=peer(1),
        device_id_type=pl.DeviceIdType.MESH,
    )
    others.wait_recv()
    grad_out[...] = scaling * jnp.sum(slots_ref[...], axis=0)[:, : grad_out.shape[1]]
    others.wait_send()
    sent(NOW, now_in)
    for level in (TWO, W3, W2):
        sent(level, field_ref.at[level])
    prior_copy.wait()
    now_copy.wait()


def write(prior_in, now_in, grad_in, prior_out, now_out, grad_out):
    prior_out[...] = prior_in[...]
    now_out[...] = now_in[...]
    grad_out[...] = grad_in[...]


def local(
    sizes,
    pressure_prior,
    pressure_now,
    adjoint_end,
    adjoint_near,
    wall_faces,
    material_ids,
    admittance,
    receivers,
    targets,
):
    shape = pressure_now.shape
    span_x, span_y, span_z = shape
    count = math.prod(sizes)
    kinds = admittance.shape[0]
    scaling = 16.0 / math.sqrt(pressure_now.size * count)
    in_hbm = pl.BlockSpec(memory_space=pltpu.HBM)
    in_vmem = pl.BlockSpec(memory_space=pltpu.VMEM)
    block = pltpu.VMEM(shape, jnp.float32)
    prior_out, now_out, grad = pl.pallas_call(
        functools.partial(kernel, sizes, scaling),
        out_shape=(
            jax.ShapeDtypeStruct(shape, jnp.float32),
            jax.ShapeDtypeStruct(shape, jnp.float32),
            jax.ShapeDtypeStruct((1, kinds), jnp.float32),
        ),
        in_specs=[in_hbm] * 6 + [in_vmem] * 3,
        out_specs=(in_hbm, in_hbm, in_vmem),
        scratch_shapes=[
            block,
            block,
            block,
            block,
            pltpu.VMEM(shape, jnp.int32),
            pltpu.VMEM(shape, jnp.int32),
            pltpu.VMEM((4,) + shape, jnp.float32),
            pltpu.VMEM((2,) + shape, jnp.float32),
            pltpu.VMEM((kinds, 8, 128), jnp.float32),
            pltpu.VMEM((count, 1, 128), jnp.float32),
            pltpu.VMEM((4, 2, span_y, span_z), jnp.float32),
            pltpu.VMEM((4, 2, span_x, 8, span_z), jnp.float32),
            pltpu.VMEM((4, span_x, span_y, span_z // 2), jnp.float32),
            pltpu.SemaphoreType.DMA((6,)),
            pltpu.SemaphoreType.DMA((2,)),
            pltpu.SemaphoreType.DMA((4, 5)),
            pltpu.SemaphoreType.DMA((4, 5)),
            pltpu.SemaphoreType.DMA((2,)),
        ],
        compiler_params=pltpu.CompilerParams(
            collective_id=0, has_side_effects=True, vmem_limit_bytes=VMEM_BYTES
        ),
    )(
        pressure_now,
        pressure_prior,
        adjoint_end,
        adjoint_near,
        wall_faces,
        material_ids,
        admittance.reshape(1, kinds),
        receivers.T,
        targets.T,
    )
    results = (prior_out, now_out, grad)
    prior_out, now_out, grad = pl.pallas_call(
        write,
        out_shape=(
            jax.ShapeDtypeStruct(shape, jnp.float32),
            jax.ShapeDtypeStruct(shape, jnp.float32),
            jax.ShapeDtypeStruct((1, kinds), jnp.float32),
        ),
        in_specs=[in_vmem] * 3,
        out_specs=(in_vmem,) * 3,
        compiler_params=pltpu.CompilerParams(vmem_limit_bytes=VMEM_BYTES),
    )(*results)
    return prior_out, now_out, grad.reshape(kinds)


def solution(mesh):
    cells = P(("rooms", "gx"), "gy", "gz")
    sizes = tuple(mesh.shape[axis] for axis in ("gx", "gy", "gz"))
    return jax.shard_map(
        functools.partial(local, sizes),
        mesh=mesh,
        in_specs=(cells,) * 6 + (P(), P("rooms", None), P("rooms", None)),
        out_specs=(cells, cells, P("rooms")),
        check_vma=False,
    )
```

```python
import functools
import math

import jax
import jax.numpy as jnp
from jax import lax
from jax.experimental import pallas as pl
from jax.experimental.pallas import tpu as pltpu
from jax.sharding import PartitionSpec as P

VMEM_BYTES = 64 * 1024 * 1024
HIGHEST = lax.Precision.HIGHEST
PRIOR, LOSS, W3, W2 = range(4)


def kernel(
    sizes,
    scaling,
    now_in,
    prior_in,
    end_in,
    near_in,
    wall_in,
    ids_in,
    table_ref,
    receivers_ref,
    targets_ref,
    prior_out,
    now_out,
    grad_out,
    now_ref,
    prior_ref,
    end_ref,
    near_ref,
    wall_ref,
    ids_ref,
    field_ref,
    result_ref,
    bins_ref,
    slots_ref,
    hx,
    hy,
    hz,
    near_x,
    near_y,
    near_z,
    near_xy,
    near_xz,
    near_yz,
    in_sems,
    out_sems,
    send_sems,
    recv_sems,
    sum_sems,
    wide_send_sems,
    wide_recv_sems,
):
    nx, ny, nz = sizes
    count = nx * ny * nz
    ix, iy, iz = lax.axis_index("gx"), lax.axis_index("gy"), lax.axis_index("gz")
    me = (ix * ny + iy) * nz + iz
    span_x, span_y, span_z = now_ref.shape
    rows = span_x * span_y
    half = span_z // 2

    def peer(step):
        other = lax.rem(me + step, count)
        return {
            "gx": other // (ny * nz),
            "gy": lax.rem(other // nz, ny),
            "gz": lax.rem(other, nz),
        }

    loads = [
        pltpu.make_async_copy(source, target, in_sems.at[i])
        for i, (source, target) in enumerate(
            (
                (ids_in, ids_ref),
                (wall_in, wall_ref),
                (now_in, now_ref),
                (prior_in, prior_ref),
                (end_in, end_ref),
                (near_in, near_ref),
            )
        )
    ]
    barrier = pltpu.get_barrier_semaphore()

    @pl.loop(1, count)
    def _(step):
        pl.semaphore_signal(
            barrier, inc=1, device_id=peer(step), device_id_type=pl.DeviceIdType.MESH
        )

    for load in loads:
        load.start()

    pl.semaphore_wait(barrier, count - 1)

    def links(level, source):
        def copy(part, target, way, where):
            return pltpu.make_async_remote_copy(
                src_ref=part,
                dst_ref=target,
                send_sem=send_sems.at[level, way],
                recv_sem=recv_sems.at[level, way],
                device_id=where,
                device_id_type=pl.DeviceIdType.MESH,
            )

        last = span_x - 1
        return (
            (copy(source.at[last], hx.at[level, 0], 0, {"gx": ix + 1}), ix < nx - 1, ix > 0),
            (copy(source.at[0], hx.at[level, 1], 1, {"gx": ix - 1}), ix > 0, ix < nx - 1),
            (
                copy(source.at[:, pl.ds(span_y - 8, 8), :], hy.at[level, 0], 2, {"gy": iy + 1}),
                iy < ny - 1,
                iy > 0,
            ),
            (
                copy(source.at[:, pl.ds(0, 8), :], hy.at[level, 1], 3, {"gy": iy - 1}),
                iy > 0,
                iy < ny - 1,
            ),
            (
                copy(
                    source.at[:, :, pl.ds(pl.multiple_of((1 - iz) * half, half), half)],
                    hz.at[level],
                    4,
                    {"gz": 1 - iz},
                ),
                None,
                None,
            ),
        )

    def when(test, act):
        if test is None:
            act()
        else:
            pl.when(test)(act)

    def send(level, source):
        for copy, sends, _ in links(level, source):
            when(sends, copy.start)

    def receive(level, source):
        for copy, _, receives in links(level, source):
            when(receives, copy.wait_recv)

    def sent(level, source):
        for copy, sends, _ in links(level, source):
            when(sends, copy.wait_send)

    def wide_links(source):
        sides_x = ((ix + 1, 0, span_x - 1, ix < nx - 1, ix > 0), (ix - 1, 1, 0, ix > 0, ix < nx - 1))
        sides_y = (
            (iy + 1, 0, pl.ds(span_y - 8, 8), iy < ny - 1, iy > 0),
            (iy - 1, 1, pl.ds(0, 8), iy > 0, iy < ny - 1),
        )
        lanes = pl.ds(pl.multiple_of((1 - iz) * half, half), half)
        other = 1 - iz
        plan = []
        for to_x, side, layer, sends, receives in sides_x:
            plan.append((source, near_x.at[side], {"gx": to_x}, sends, receives))
        for to_y, side, band, sends, receives in sides_y:
            plan.append((source.at[:, band, :], near_y.at[side], {"gy": to_y}, sends, receives))
        plan.append((source.at[:, :, lanes], near_z, {"gz": other}, None, None))
        for to_x, side, layer, sends, receives in sides_x:
            for to_y, side_y, band, sends_y, receives_y in sides_y:
                plan.append(
                    (
                        source.at[layer, band, :],
                        near_xy.at[side, side_y],
                        {"gx": to_x, "gy": to_y},
                        sends & sends_y,
                        receives & receives_y,
                    )
                )
            plan.append(
                (
                    source.at[layer, :, lanes],
                    near_xz.at[side],
                    {"gx": to_x, "gz": other},
                    sends,
                    receives,
                )
            )
        for to_y, side, band, sends, receives in sides_y:
            plan.append(
                (
                    source.at[:, band, lanes],
                    near_yz.at[side],
                    {"gy": to_y, "gz": other},
                    sends,
                    receives,
                )
            )
        return [
            (
                pltpu.make_async_remote_copy(
                    src_ref=part,
                    dst_ref=target,
                    send_sem=wide_send_sems.at[i],
                    recv_sem=wide_recv_sems.at[i],
                    device_id=where,
                    device_id_type=pl.DeviceIdType.MESH,
                ),
                sends,
                receives,
            )
            for i, (part, target, where, sends, receives) in enumerate(plan)
        ]

    for copy, sends, _ in wide_links(now_in):
        when(sends, copy.start)
    send(PRIOR, prior_in)

    def clear(ref):
        ref[...] = jnp.zeros(ref.shape, jnp.float32)

    for side, test in ((0, ix == 0), (1, ix == nx - 1)):

        @pl.when(test)
        def _():
            for level in range(4):
                clear(hx.at[level, side])
            for ref in (near_x, near_xy, near_xz):
                clear(ref.at[side])

    for side, test in ((0, iy == 0), (1, iy == ny - 1)):

        @pl.when(test)
        def _():
            for level in range(4):
                clear(hy.at[level, side])
            clear(near_y.at[side])
            clear(near_yz.at[side])

    for side, test in ((0, ix == 0), (1, ix == nx - 1)):
        for side_y, test_y in ((0, iy == 0), (1, iy == ny - 1)):

            @pl.when(test_y & jnp.logical_not(test))
            def _():
                clear(near_xy.at[side, side_y])

    row = lax.broadcasted_iota(jnp.int32, (rows, span_z), 0)
    lane = lax.broadcasted_iota(jnp.int32, (rows, span_z), 1)
    top = lax.rem(row, span_y) == 0
    bottom = lax.rem(row, span_y) == span_y - 1

    def across_y(field, before, after, first, last):
        before = jnp.where(first, before, pltpu.roll(field, 1, 0))
        return before + jnp.where(last, after, pltpu.roll(field, field.shape[0] - 1, 0))

    def across_z(field, beside):
        count_rows = field.shape[0]
        before = jnp.where(iz == 1, beside[:, half - 1 :], 0.0)
        after = jnp.where(iz == 0, beside[:, :1], 0.0)
        lanes = lane[:count_rows]
        before = jnp.where(lanes == 0, before, pltpu.roll(field, 1, 1))
        return before + jnp.where(lanes == span_z - 1, after, pltpu.roll(field, span_z - 1, 1))

    def spread(line, height):
        layers, _, width = line.shape
        shape = (layers, height, width)
        return jnp.broadcast_to(line, shape).reshape(layers * height, width)

    def laplace(field, x_0, x_1, y_0, y_1, z):
        total = jnp.concatenate([x_0, field[: rows - span_y]], axis=0)
        total = total + jnp.concatenate([field[span_y:], x_1], axis=0)
        y_0, y_1 = spread(y_0[:, 7:8, :], span_y), spread(y_1[:, 0:1, :], span_y)
        total = total + across_y(field, y_0, y_1, top, bottom)
        return total + across_z(field, z) - 6.0 * field

    def halo(level):
        return (
            hx[level, 0],
            hx[level, 1],
            hy[level, 0],
            hy[level, 1],
            hz[level].reshape(rows, half),
        )

    def step(field, laplacian, loss, earlier):
        return loss * (2.0 * field + 0.25 * laplacian) - (2.0 * loss - 1.0) * earlier

    def step_beside(now):
        layers = []
        for side, nearest in ((0, 1), (1, 0)):
            centre = near_x[side, nearest]
            own = now[:span_y] if side == 0 else now[rows - span_y :]
            total = near_x[side, 1 - nearest] + own
            total = total + across_y(
                centre, near_xy[side, 0][7:8], near_xy[side, 1][0:1], top[:span_y], bottom[:span_y]
            )
            total = total + across_z(centre, near_xz[side]) - 6.0 * centre
            layers.append(step(centre, total, hx[LOSS, side], hx[PRIOR, side]))
        bands = []
        for side in range(2):
            height = span_x * 8
            centre = near_y[side].reshape(height, span_z)
            total = jnp.concatenate([near_xy[0, side], centre[: height - 8]], axis=0)
            total = total + jnp.concatenate([centre[8:], near_xy[1, side]], axis=0)
            if side == 0:
                own = spread(now_ref[:, 0:1, :], 8)
                total = total + pltpu.roll(centre, 1, 0) + own
            else:
                own = spread(now_ref[:, span_y - 1 : span_y, :], 8)
                total = total + pltpu.roll(centre, height - 1, 0) + own
            total = total + across_z(centre, near_yz[side].reshape(height, half)) - 6.0 * centre
            loss = hy[LOSS, side].reshape(height, span_z)
            earlier = hy[PRIOR, side].reshape(height, span_z)
            bands.append(step(centre, total, loss, earlier).reshape(span_x, 8, span_z))
        centre = near_z[...].reshape(rows, half)
        total = jnp.concatenate([near_xz[0], centre[: rows - span_y]], axis=0)
        total = total + jnp.concatenate([centre[span_y:], near_xz[1]], axis=0)
        y_0 = spread(near_yz[0][:, 7:8, :], span_y)
        y_1 = spread(near_yz[1][:, 0:1, :], span_y)
        total = total + across_y(centre, y_0, y_1, top[:, :half], bottom[:, :half])
        own = jnp.where(iz == 0, now[:, span_z - 1 :], now[:, :1])
        inner = jnp.where(iz == 0, pltpu.roll(centre, half - 1, 1), pltpu.roll(centre, 1, 1))
        total = total + inner + own - 6.0 * centre
        loss = hz[LOSS].reshape(rows, half)
        earlier = hz[PRIOR].reshape(rows, half)
        return (*layers, *bands, step(centre, total, loss, earlier))

    def flat(ref):
        return ref[...].reshape(rows, span_z)

    place = receivers_ref[...]
    spots = place.shape[1]
    at_x = place[0:1] - ix * span_x
    at_y = place[1:2] - iy * span_y
    at_z = place[2:3] - iz * span_z
    inside = (at_x >= 0) & (at_x < span_x) & (at_y >= 0) & (at_y < span_y)
    inside = inside & (at_z >= 0) & (at_z < span_z)
    at_row = jnp.where(inside, at_x * span_y + at_y, -1)
    in_row = lax.broadcasted_iota(jnp.int32, (rows, spots), 0) == at_row
    in_row = in_row.astype(jnp.float32)
    in_lane = lax.broadcasted_iota(jnp.int32, (span_z, spots), 0) == at_z
    in_lane = in_lane.astype(jnp.float32).astype(jnp.bfloat16)

    def exact(values, pattern, dims):
        parts = []
        rest = values
        for _ in range(3):
            part = rest.astype(jnp.bfloat16)
            rest = rest - part.astype(jnp.float32)
            parts.append(part)
        product = lax.dot_general(
            jnp.concatenate(parts, axis=0), pattern, (dims, ((), ())),
            preferred_element_type=jnp.float32,
        )
        high, middle, low = jnp.split(product, 3, axis=0)
        return high + (middle + low)

    def misfit(field, column):
        lines = exact(field, in_lane, ((1,), (0,)))
        values = jnp.sum(lines * in_row, axis=0, keepdims=True)
        mismatch = jnp.where(inside, values - targets_ref[column : column + 1], 0.0)
        return exact(in_row * mismatch, in_lane, ((1,), (1,)))

    for load in loads[:2]:
        load.wait()
    ids = flat(ids_ref)
    walls = 0.5 * flat(wall_ref).astype(jnp.float32)
    table = table_ref[...]
    table = jnp.broadcast_to(jnp.concatenate([table, table], axis=1), (rows, 128))
    rate = jnp.concatenate(
        [
            jnp.take_along_axis(table, ids[:, i : i + 128], axis=1, mode="promise_in_bounds")
            for i in range(0, span_z, 128)
        ],
        axis=1,
    )
    inverse_loss = 1.0 / (1.0 + walls * rate)
    reflect = 2.0 * inverse_loss - 1.0

    field_ref[LOSS] = inverse_loss.reshape(now_ref.shape)
    send(LOSS, field_ref.at[LOSS])

    for load in loads[2:]:
        load.wait()
    now = flat(now_ref)
    prior = flat(prior_ref)
    wide = wide_links(now_in)
    for copy, _, receives in wide[:5]:
        when(receives, copy.wait_recv)
    around = (near_x[0, 1], near_x[1, 0], near_y[0], near_y[1], near_z[...].reshape(rows, half))
    two = step(now, laplace(now, *around), inverse_loss, prior)
    for copy, _, receives in wide[5:]:
        when(receives, copy.wait_recv)

    receive(PRIOR, prior_in)
    receive(LOSS, field_ref.at[LOSS])
    three = step(two, laplace(two, *step_beside(now)), inverse_loss, now)
    adjoint_three = flat(end_ref) + misfit(three, 1)
    weighted_three = inverse_loss * adjoint_three
    field_ref[W3] = weighted_three.reshape(now_ref.shape)
    send(W3, field_ref.at[W3])
    term_three = weighted_three * (now - three)
    incoming = flat(near_ref) + misfit(two, 0)

    receive(W3, field_ref.at[W3])
    adjoint_two = incoming + 2.0 * weighted_three + 0.25 * laplace(weighted_three, *halo(W3))
    weighted_two = inverse_loss * adjoint_two
    field_ref[W2] = weighted_two.reshape(now_ref.shape)
    send(W2, field_ref.at[W2])

    terms = walls * (term_three + weighted_two * (prior - two))
    kinds = bins_ref.shape[0]

    @pl.loop(0, kinds, unroll=8)
    def _(kind):
        mine = jnp.where(ids == kind, terms, 0.0)
        mine = jnp.sum(mine.reshape(rows // 8, 8, span_z), axis=0)
        bins_ref[kind] = mine[:, :128] + mine[:, 128:]

    bins = jnp.sum(bins_ref[...], axis=1)
    ones = jnp.ones((8, 128), jnp.float32)
    sums = lax.dot_general(
        ones, bins, (((1,), (1,)), ((), ())), precision=HIGHEST,
        preferred_element_type=jnp.float32,
    )
    slots_ref[me] = jnp.concatenate([sums[:1], sums[:1]], axis=1)

    @pl.loop(1, count)
    def _(step):
        pltpu.make_async_remote_copy(
            src_ref=slots_ref.at[me],
            dst_ref=slots_ref.at[me],
            send_sem=sum_sems.at[0],
            recv_sem=sum_sems.at[1],
            device_id=peer(step),
            device_id_type=pl.DeviceIdType.MESH,
        ).start()

    result_ref[0] = (-reflect * adjoint_two).reshape(now_ref.shape)
    prior_copy = pltpu.make_async_copy(result_ref.at[0], prior_out, out_sems.at[0])
    prior_copy.start()

    receive(W2, field_ref.at[W2])
    result = -reflect * adjoint_three + 2.0 * weighted_two + 0.25 * laplace(weighted_two, *halo(W2))
    result_ref[1] = result.reshape(now_ref.shape)
    now_copy = pltpu.make_async_copy(result_ref.at[1], now_out, out_sems.at[1])
    now_copy.start()

    others = pltpu.make_async_remote_copy(
        src_ref=slots_ref.at[pl.ds(0, count - 1)],
        dst_ref=slots_ref.at[pl.ds(0, count - 1)],
        send_sem=sum_sems.at[0],
        recv_sem=sum_sems.at[1],
        device_id=peer(1),
        device_id_type=pl.DeviceIdType.MESH,
    )
    others.wait_recv()
    grad_out[...] = scaling * jnp.sum(slots_ref[...], axis=0)[:, : grad_out.shape[1]]
    others.wait_send()
    for copy, sends, _ in wide_links(now_in):
        when(sends, copy.wait_send)
    sent(PRIOR, prior_in)
    for level in (LOSS, W3, W2):
        sent(level, field_ref.at[level])
    prior_copy.wait()
    now_copy.wait()


def write(prior_in, now_in, grad_in, prior_out, now_out, grad_out):
    prior_out[...] = prior_in[...]
    now_out[...] = now_in[...]
    grad_out[...] = grad_in[...]


def local(
    sizes,
    pressure_prior,
    pressure_now,
    adjoint_end,
    adjoint_near,
    wall_faces,
    material_ids,
    admittance,
    receivers,
    targets,
):
    shape = pressure_now.shape
    span_x, span_y, span_z = shape
    count = math.prod(sizes)
    kinds = admittance.shape[0]
    scaling = 16.0 / math.sqrt(pressure_now.size * count)
    in_hbm = pl.BlockSpec(memory_space=pltpu.HBM)
    in_vmem = pl.BlockSpec(memory_space=pltpu.VMEM)
    block = pltpu.VMEM(shape, jnp.float32)
    prior_out, now_out, grad = pl.pallas_call(
        functools.partial(kernel, sizes, scaling),
        out_shape=(
            jax.ShapeDtypeStruct(shape, jnp.float32),
            jax.ShapeDtypeStruct(shape, jnp.float32),
            jax.ShapeDtypeStruct((1, kinds), jnp.float32),
        ),
        in_specs=[in_hbm] * 6 + [in_vmem] * 3,
        out_specs=(in_hbm, in_hbm, in_vmem),
        scratch_shapes=[
            block,
            block,
            block,
            block,
            pltpu.VMEM(shape, jnp.int32),
            pltpu.VMEM(shape, jnp.int32),
            pltpu.VMEM((4,) + shape, jnp.float32),
            pltpu.VMEM((2,) + shape, jnp.float32),
            pltpu.VMEM((kinds, 8, 128), jnp.float32),
            pltpu.VMEM((count, 1, 128), jnp.float32),
            pltpu.VMEM((4, 2, span_y, span_z), jnp.float32),
            pltpu.VMEM((4, 2, span_x, 8, span_z), jnp.float32),
            pltpu.VMEM((4, span_x, span_y, span_z // 2), jnp.float32),
            pltpu.VMEM((2,) + shape, jnp.float32),
            pltpu.VMEM((2, span_x, 8, span_z), jnp.float32),
            pltpu.VMEM((span_x, span_y, span_z // 2), jnp.float32),
            pltpu.VMEM((2, 2, 8, span_z), jnp.float32),
            pltpu.VMEM((2, span_y, span_z // 2), jnp.float32),
            pltpu.VMEM((2, span_x, 8, span_z // 2), jnp.float32),
            pltpu.SemaphoreType.DMA((6,)),
            pltpu.SemaphoreType.DMA((2,)),
            pltpu.SemaphoreType.DMA((4, 5)),
            pltpu.SemaphoreType.DMA((4, 5)),
            pltpu.SemaphoreType.DMA((2,)),
            pltpu.SemaphoreType.DMA((13,)),
            pltpu.SemaphoreType.DMA((13,)),
        ],
        compiler_params=pltpu.CompilerParams(
            collective_id=0, has_side_effects=True, vmem_limit_bytes=VMEM_BYTES
        ),
    )(
        pressure_now,
        pressure_prior,
        adjoint_end,
        adjoint_near,
        wall_faces,
        material_ids,
        admittance.reshape(1, kinds),
        receivers.T,
        targets.T,
    )
    results = (prior_out, now_out, grad)
    prior_out, now_out, grad = pl.pallas_call(
        write,
        out_shape=(
            jax.ShapeDtypeStruct(shape, jnp.float32),
            jax.ShapeDtypeStruct(shape, jnp.float32),
            jax.ShapeDtypeStruct((1, kinds), jnp.float32),
        ),
        in_specs=[in_vmem] * 3,
        out_specs=(in_vmem,) * 3,
        compiler_params=pltpu.CompilerParams(vmem_limit_bytes=VMEM_BYTES),
    )(*results)
    return prior_out, now_out, grad.reshape(kinds)


def solution(mesh):
    cells = P(("rooms", "gx"), "gy", "gz")
    sizes = tuple(mesh.shape[axis] for axis in ("gx", "gy", "gz"))
    return jax.shard_map(
        functools.partial(local, sizes),
        mesh=mesh,
        in_specs=(cells,) * 6 + (P(), P("rooms", None), P("rooms", None)),
        out_specs=(cells, cells, P("rooms")),
        check_vma=False,
    )
```

```python
import functools
import math

import jax
import jax.numpy as jnp
from jax import lax
from jax.experimental import pallas as pl
from jax.experimental.pallas import tpu as pltpu
from jax.sharding import PartitionSpec as P

VMEM_BYTES = 64 * 1024 * 1024
HIGHEST = lax.Precision.HIGHEST
PRIOR, LOSS, W3, W2 = range(4)


def kernel(
    sizes,
    scaling,
    now_in,
    prior_in,
    end_in,
    near_in,
    wall_in,
    ids_in,
    table_in,
    receivers_in,
    targets_in,
    prior_out,
    now_out,
    grad_out,
    now_ref,
    prior_ref,
    end_ref,
    near_ref,
    wall_ref,
    ids_ref,
    table_ref,
    receivers_ref,
    targets_ref,
    field_ref,
    result_ref,
    grad_ref,
    bins_ref,
    slots_ref,
    hx,
    hy,
    hz,
    near_x,
    near_y,
    near_z,
    near_xy,
    near_xz,
    near_yz,
    in_sems,
    out_sems,
    send_sems,
    recv_sems,
    sum_sems,
    wide_send_sems,
    wide_recv_sems,
):
    nx, ny, nz = sizes
    count = nx * ny * nz
    ix, iy, iz = lax.axis_index("gx"), lax.axis_index("gy"), lax.axis_index("gz")
    me = (ix * ny + iy) * nz + iz
    span_x, span_y, span_z = now_ref.shape
    rows = span_x * span_y
    half = span_z // 2

    def peer(step):
        other = lax.rem(me + step, count)
        return {
            "gx": other // (ny * nz),
            "gy": lax.rem(other // nz, ny),
            "gz": lax.rem(other, nz),
        }

    loads = [
        pltpu.make_async_copy(source, target, in_sems.at[i])
        for i, (source, target) in enumerate(
            (
                (ids_in, ids_ref),
                (wall_in, wall_ref),
                (table_in, table_ref),
                (receivers_in, receivers_ref),
                (targets_in, targets_ref),
                (now_in, now_ref),
                (prior_in, prior_ref),
                (end_in, end_ref),
                (near_in, near_ref),
            )
        )
    ]
    barrier = pltpu.get_barrier_semaphore()

    @pl.loop(1, count)
    def _(step):
        pl.semaphore_signal(
            barrier, inc=1, device_id=peer(step), device_id_type=pl.DeviceIdType.MESH
        )

    for load in loads:
        load.start()

    pl.semaphore_wait(barrier, count - 1)

    def links(level, source):
        def copy(part, target, way, where):
            return pltpu.make_async_remote_copy(
                src_ref=part,
                dst_ref=target,
                send_sem=send_sems.at[level, way],
                recv_sem=recv_sems.at[level, way],
                device_id=where,
                device_id_type=pl.DeviceIdType.MESH,
            )

        last = span_x - 1
        return (
            (copy(source.at[last], hx.at[level, 0], 0, {"gx": ix + 1}), ix < nx - 1, ix > 0),
            (copy(source.at[0], hx.at[level, 1], 1, {"gx": ix - 1}), ix > 0, ix < nx - 1),
            (
                copy(source.at[:, pl.ds(span_y - 8, 8), :], hy.at[level, 0], 2, {"gy": iy + 1}),
                iy < ny - 1,
                iy > 0,
            ),
            (
                copy(source.at[:, pl.ds(0, 8), :], hy.at[level, 1], 3, {"gy": iy - 1}),
                iy > 0,
                iy < ny - 1,
            ),
            (
                copy(
                    source.at[:, :, pl.ds(pl.multiple_of((1 - iz) * half, half), half)],
                    hz.at[level],
                    4,
                    {"gz": 1 - iz},
                ),
                None,
                None,
            ),
        )

    def when(test, act):
        if test is None:
            act()
        else:
            pl.when(test)(act)

    def send(level, source):
        for copy, sends, _ in links(level, source):
            when(sends, copy.start)

    def receive(level, source):
        for copy, _, receives in links(level, source):
            when(receives, copy.wait_recv)

    def sent(level, source):
        for copy, sends, _ in links(level, source):
            when(sends, copy.wait_send)

    def wide_links(source):
        sides_x = ((ix + 1, 0, span_x - 1, ix < nx - 1, ix > 0), (ix - 1, 1, 0, ix > 0, ix < nx - 1))
        sides_y = (
            (iy + 1, 0, pl.ds(span_y - 8, 8), iy < ny - 1, iy > 0),
            (iy - 1, 1, pl.ds(0, 8), iy > 0, iy < ny - 1),
        )
        lanes = pl.ds(pl.multiple_of((1 - iz) * half, half), half)
        other = 1 - iz
        plan = []
        for to_x, side, layer, sends, receives in sides_x:
            plan.append((source, near_x.at[side], {"gx": to_x}, sends, receives))
        for to_y, side, band, sends, receives in sides_y:
            plan.append((source.at[:, band, :], near_y.at[side], {"gy": to_y}, sends, receives))
        plan.append((source.at[:, :, lanes], near_z, {"gz": other}, None, None))
        for to_x, side, layer, sends, receives in sides_x:
            for to_y, side_y, band, sends_y, receives_y in sides_y:
                plan.append(
                    (
                        source.at[layer, band, :],
                        near_xy.at[side, side_y],
                        {"gx": to_x, "gy": to_y},
                        sends & sends_y,
                        receives & receives_y,
                    )
                )
            plan.append(
                (
                    source.at[layer, :, lanes],
                    near_xz.at[side],
                    {"gx": to_x, "gz": other},
                    sends,
                    receives,
                )
            )
        for to_y, side, band, sends, receives in sides_y:
            plan.append(
                (
                    source.at[:, band, lanes],
                    near_yz.at[side],
                    {"gy": to_y, "gz": other},
                    sends,
                    receives,
                )
            )
        return [
            (
                pltpu.make_async_remote_copy(
                    src_ref=part,
                    dst_ref=target,
                    send_sem=wide_send_sems.at[i],
                    recv_sem=wide_recv_sems.at[i],
                    device_id=where,
                    device_id_type=pl.DeviceIdType.MESH,
                ),
                sends,
                receives,
            )
            for i, (part, target, where, sends, receives) in enumerate(plan)
        ]

    for copy, sends, _ in wide_links(now_in):
        when(sends, copy.start)
    send(PRIOR, prior_in)

    def clear(ref):
        ref[...] = jnp.zeros(ref.shape, jnp.float32)

    for side, test in ((0, ix == 0), (1, ix == nx - 1)):

        @pl.when(test)
        def _():
            for level in range(4):
                clear(hx.at[level, side])
            for ref in (near_x, near_xy, near_xz):
                clear(ref.at[side])

    for side, test in ((0, iy == 0), (1, iy == ny - 1)):

        @pl.when(test)
        def _():
            for level in range(4):
                clear(hy.at[level, side])
            clear(near_y.at[side])
            clear(near_yz.at[side])

    for side, test in ((0, ix == 0), (1, ix == nx - 1)):
        for side_y, test_y in ((0, iy == 0), (1, iy == ny - 1)):

            @pl.when(test_y & jnp.logical_not(test))
            def _():
                clear(near_xy.at[side, side_y])

    row = lax.broadcasted_iota(jnp.int32, (rows, span_z), 0)
    lane = lax.broadcasted_iota(jnp.int32, (rows, span_z), 1)
    top = lax.rem(row, span_y) == 0
    bottom = lax.rem(row, span_y) == span_y - 1

    def across_y(field, before, after, first, last):
        before = jnp.where(first, before, pltpu.roll(field, 1, 0))
        return before + jnp.where(last, after, pltpu.roll(field, field.shape[0] - 1, 0))

    def across_z(field, beside):
        count_rows = field.shape[0]
        before = jnp.where(iz == 1, beside[:, half - 1 :], 0.0)
        after = jnp.where(iz == 0, beside[:, :1], 0.0)
        lanes = lane[:count_rows]
        before = jnp.where(lanes == 0, before, pltpu.roll(field, 1, 1))
        return before + jnp.where(lanes == span_z - 1, after, pltpu.roll(field, span_z - 1, 1))

    def spread(line, height):
        layers, _, width = line.shape
        shape = (layers, height, width)
        return jnp.broadcast_to(line, shape).reshape(layers * height, width)

    def laplace(field, x_0, x_1, y_0, y_1, z):
        total = jnp.concatenate([x_0, field[: rows - span_y]], axis=0)
        total = total + jnp.concatenate([field[span_y:], x_1], axis=0)
        y_0, y_1 = spread(y_0[:, 7:8, :], span_y), spread(y_1[:, 0:1, :], span_y)
        total = total + across_y(field, y_0, y_1, top, bottom)
        return total + across_z(field, z) - 6.0 * field

    def halo(level):
        return (
            hx[level, 0],
            hx[level, 1],
            hy[level, 0],
            hy[level, 1],
            hz[level].reshape(rows, half),
        )

    def step(field, laplacian, loss, earlier):
        return loss * (2.0 * field + 0.25 * laplacian) - (2.0 * loss - 1.0) * earlier

    def step_beside(now):
        layers = []
        for side, nearest in ((0, 1), (1, 0)):
            centre = near_x[side, nearest]
            own = now[:span_y] if side == 0 else now[rows - span_y :]
            total = near_x[side, 1 - nearest] + own
            total = total + across_y(
                centre, near_xy[side, 0][7:8], near_xy[side, 1][0:1], top[:span_y], bottom[:span_y]
            )
            total = total + across_z(centre, near_xz[side]) - 6.0 * centre
            layers.append(step(centre, total, hx[LOSS, side], hx[PRIOR, side]))
        bands = []
        for side in range(2):
            height = span_x * 8
            centre = near_y[side].reshape(height, span_z)
            total = jnp.concatenate([near_xy[0, side], centre[: height - 8]], axis=0)
            total = total + jnp.concatenate([centre[8:], near_xy[1, side]], axis=0)
            if side == 0:
                own = spread(now_ref[:, 0:1, :], 8)
                total = total + pltpu.roll(centre, 1, 0) + own
            else:
                own = spread(now_ref[:, span_y - 1 : span_y, :], 8)
                total = total + pltpu.roll(centre, height - 1, 0) + own
            total = total + across_z(centre, near_yz[side].reshape(height, half)) - 6.0 * centre
            loss = hy[LOSS, side].reshape(height, span_z)
            earlier = hy[PRIOR, side].reshape(height, span_z)
            bands.append(step(centre, total, loss, earlier).reshape(span_x, 8, span_z))
        centre = near_z[...].reshape(rows, half)
        total = jnp.concatenate([near_xz[0], centre[: rows - span_y]], axis=0)
        total = total + jnp.concatenate([centre[span_y:], near_xz[1]], axis=0)
        y_0 = spread(near_yz[0][:, 7:8, :], span_y)
        y_1 = spread(near_yz[1][:, 0:1, :], span_y)
        total = total + across_y(centre, y_0, y_1, top[:, :half], bottom[:, :half])
        own = jnp.where(iz == 0, now[:, span_z - 1 :], now[:, :1])
        inner = jnp.where(iz == 0, pltpu.roll(centre, half - 1, 1), pltpu.roll(centre, 1, 1))
        total = total + inner + own - 6.0 * centre
        loss = hz[LOSS].reshape(rows, half)
        earlier = hz[PRIOR].reshape(rows, half)
        return (*layers, *bands, step(centre, total, loss, earlier))

    def flat(ref):
        return ref[...].reshape(rows, span_z)

    for load in loads[:5]:
        load.wait()

    place = receivers_ref[...]
    spots = place.shape[1]
    at_x = place[0:1] - ix * span_x
    at_y = place[1:2] - iy * span_y
    at_z = place[2:3] - iz * span_z
    inside = (at_x >= 0) & (at_x < span_x) & (at_y >= 0) & (at_y < span_y)
    inside = inside & (at_z >= 0) & (at_z < span_z)
    at_row = jnp.where(inside, at_x * span_y + at_y, -1)
    in_row = lax.broadcasted_iota(jnp.int32, (rows, spots), 0) == at_row
    in_row = in_row.astype(jnp.float32)
    in_lane = lax.broadcasted_iota(jnp.int32, (span_z, spots), 0) == at_z
    in_lane = in_lane.astype(jnp.float32).astype(jnp.bfloat16)

    def exact(values, pattern, dims):
        parts = []
        rest = values
        for _ in range(3):
            part = rest.astype(jnp.bfloat16)
            rest = rest - part.astype(jnp.float32)
            parts.append(part)
        product = lax.dot_general(
            jnp.concatenate(parts, axis=0), pattern, (dims, ((), ())),
            preferred_element_type=jnp.float32,
        )
        high, middle, low = jnp.split(product, 3, axis=0)
        return high + (middle + low)

    def misfit(field, column):
        lines = exact(field, in_lane, ((1,), (0,)))
        values = jnp.sum(lines * in_row, axis=0, keepdims=True)
        mismatch = jnp.where(inside, values - targets_ref[column : column + 1], 0.0)
        return exact(in_row * mismatch, in_lane, ((1,), (1,)))

    ids = flat(ids_ref)
    walls = 0.5 * flat(wall_ref).astype(jnp.float32)
    table = table_ref[...]
    table = jnp.broadcast_to(jnp.concatenate([table, table], axis=1), (rows, 128))
    rate = jnp.concatenate(
        [
            jnp.take_along_axis(table, ids[:, i : i + 128], axis=1, mode="promise_in_bounds")
            for i in range(0, span_z, 128)
        ],
        axis=1,
    )
    inverse_loss = 1.0 / (1.0 + walls * rate)
    reflect = 2.0 * inverse_loss - 1.0

    field_ref[LOSS] = inverse_loss.reshape(now_ref.shape)
    send(LOSS, field_ref.at[LOSS])

    for load in loads[5:]:
        load.wait()
    now = flat(now_ref)
    prior = flat(prior_ref)
    wide = wide_links(now_in)
    for copy, _, receives in wide[:5]:
        when(receives, copy.wait_recv)
    around = (near_x[0, 1], near_x[1, 0], near_y[0], near_y[1], near_z[...].reshape(rows, half))
    two = step(now, laplace(now, *around), inverse_loss, prior)
    for copy, _, receives in wide[5:]:
        when(receives, copy.wait_recv)

    receive(PRIOR, prior_in)
    receive(LOSS, field_ref.at[LOSS])
    three = step(two, laplace(two, *step_beside(now)), inverse_loss, now)
    adjoint_three = flat(end_ref) + misfit(three, 1)
    weighted_three = inverse_loss * adjoint_three
    field_ref[W3] = weighted_three.reshape(now_ref.shape)
    send(W3, field_ref.at[W3])
    term_three = weighted_three * (now - three)
    incoming = flat(near_ref) + misfit(two, 0)

    receive(W3, field_ref.at[W3])
    adjoint_two = incoming + 2.0 * weighted_three + 0.25 * laplace(weighted_three, *halo(W3))
    weighted_two = inverse_loss * adjoint_two
    field_ref[W2] = weighted_two.reshape(now_ref.shape)
    send(W2, field_ref.at[W2])

    terms = walls * (term_three + weighted_two * (prior - two))
    kinds = bins_ref.shape[0]

    @pl.loop(0, kinds, unroll=8)
    def _(kind):
        mine = jnp.where(ids == kind, terms, 0.0)
        mine = jnp.sum(mine.reshape(rows // 8, 8, span_z), axis=0)
        bins_ref[kind] = mine[:, :128] + mine[:, 128:]

    bins = jnp.sum(bins_ref[...], axis=1)
    ones = jnp.ones((8, 128), jnp.float32)
    sums = lax.dot_general(
        ones, bins, (((1,), (1,)), ((), ())), precision=HIGHEST,
        preferred_element_type=jnp.float32,
    )
    slots_ref[me] = jnp.concatenate([sums[:1], sums[:1]], axis=1)

    @pl.loop(1, count)
    def _(step):
        pltpu.make_async_remote_copy(
            src_ref=slots_ref.at[me],
            dst_ref=slots_ref.at[me],
            send_sem=sum_sems.at[0],
            recv_sem=sum_sems.at[1],
            device_id=peer(step),
            device_id_type=pl.DeviceIdType.MESH,
        ).start()

    result_ref[0] = (-reflect * adjoint_two).reshape(now_ref.shape)
    prior_copy = pltpu.make_async_copy(result_ref.at[0], prior_out, out_sems.at[0])
    prior_copy.start()

    receive(W2, field_ref.at[W2])
    result = -reflect * adjoint_three + 2.0 * weighted_two + 0.25 * laplace(weighted_two, *halo(W2))
    result_ref[1] = result.reshape(now_ref.shape)
    now_copy = pltpu.make_async_copy(result_ref.at[1], now_out, out_sems.at[1])
    now_copy.start()

    others = pltpu.make_async_remote_copy(
        src_ref=slots_ref.at[pl.ds(0, count - 1)],
        dst_ref=slots_ref.at[pl.ds(0, count - 1)],
        send_sem=sum_sems.at[0],
        recv_sem=sum_sems.at[1],
        device_id=peer(1),
        device_id_type=pl.DeviceIdType.MESH,
    )
    others.wait_recv()
    grad_ref[...] = scaling * jnp.sum(slots_ref[...], axis=0)[:, : grad_ref.shape[1]]
    grad_copy = pltpu.make_async_copy(grad_ref, grad_out, out_sems.at[2])
    grad_copy.start()
    others.wait_send()
    for copy, sends, _ in wide_links(now_in):
        when(sends, copy.wait_send)
    sent(PRIOR, prior_in)
    for level in (LOSS, W3, W2):
        sent(level, field_ref.at[level])
    prior_copy.wait()
    now_copy.wait()
    grad_copy.wait()


def write(prior_in, now_in, grad_in, prior_out, now_out, grad_out):
    prior_out[...] = prior_in[...]
    now_out[...] = now_in[...]
    grad_out[...] = grad_in[...]


def local(
    sizes,
    pressure_prior,
    pressure_now,
    adjoint_end,
    adjoint_near,
    wall_faces,
    material_ids,
    admittance,
    receivers,
    targets,
):
    shape = pressure_now.shape
    span_x, span_y, span_z = shape
    count = math.prod(sizes)
    kinds = admittance.shape[0]
    scaling = 16.0 / math.sqrt(pressure_now.size * count)
    in_hbm = pl.BlockSpec(memory_space=pltpu.HBM)
    in_vmem = pl.BlockSpec(memory_space=pltpu.VMEM)
    block = pltpu.VMEM(shape, jnp.float32)
    prior_out, now_out, grad = pl.pallas_call(
        functools.partial(kernel, sizes, scaling),
        out_shape=(
            jax.ShapeDtypeStruct(shape, jnp.float32),
            jax.ShapeDtypeStruct(shape, jnp.float32),
            jax.ShapeDtypeStruct((1, kinds), jnp.float32),
        ),
        in_specs=[in_hbm] * 9,
        out_specs=(in_hbm,) * 3,
        scratch_shapes=[
            block,
            block,
            block,
            block,
            pltpu.VMEM(shape, jnp.int32),
            pltpu.VMEM(shape, jnp.int32),
            pltpu.VMEM((1, kinds), jnp.float32),
            pltpu.VMEM(receivers.shape[::-1], jnp.int32),
            pltpu.VMEM(targets.shape[::-1], jnp.float32),
            pltpu.VMEM((4,) + shape, jnp.float32),
            pltpu.VMEM((2,) + shape, jnp.float32),
            pltpu.VMEM((1, kinds), jnp.float32),
            pltpu.VMEM((kinds, 8, 128), jnp.float32),
            pltpu.VMEM((count, 1, 128), jnp.float32),
            pltpu.VMEM((4, 2, span_y, span_z), jnp.float32),
            pltpu.VMEM((4, 2, span_x, 8, span_z), jnp.float32),
            pltpu.VMEM((4, span_x, span_y, span_z // 2), jnp.float32),
            pltpu.VMEM((2,) + shape, jnp.float32),
            pltpu.VMEM((2, span_x, 8, span_z), jnp.float32),
            pltpu.VMEM((span_x, span_y, span_z // 2), jnp.float32),
            pltpu.VMEM((2, 2, 8, span_z), jnp.float32),
            pltpu.VMEM((2, span_y, span_z // 2), jnp.float32),
            pltpu.VMEM((2, span_x, 8, span_z // 2), jnp.float32),
            pltpu.SemaphoreType.DMA((9,)),
            pltpu.SemaphoreType.DMA((3,)),
            pltpu.SemaphoreType.DMA((4, 5)),
            pltpu.SemaphoreType.DMA((4, 5)),
            pltpu.SemaphoreType.DMA((2,)),
            pltpu.SemaphoreType.DMA((13,)),
            pltpu.SemaphoreType.DMA((13,)),
        ],
        compiler_params=pltpu.CompilerParams(
            collective_id=0, has_side_effects=True, vmem_limit_bytes=VMEM_BYTES
        ),
    )(
        pressure_now,
        pressure_prior,
        adjoint_end,
        adjoint_near,
        wall_faces,
        material_ids,
        admittance.reshape(1, kinds),
        receivers.T,
        targets.T,
    )
    results = (prior_out, now_out, grad)
    prior_out, now_out, grad = pl.pallas_call(
        write,
        out_shape=(
            jax.ShapeDtypeStruct(shape, jnp.float32),
            jax.ShapeDtypeStruct(shape, jnp.float32),
            jax.ShapeDtypeStruct((1, kinds), jnp.float32),
        ),
        in_specs=[in_vmem] * 3,
        out_specs=(in_vmem,) * 3,
        compiler_params=pltpu.CompilerParams(vmem_limit_bytes=VMEM_BYTES),
    )(*results)
    return prior_out, now_out, grad.reshape(kinds)


def solution(mesh):
    cells = P(("rooms", "gx"), "gy", "gz")
    sizes = tuple(mesh.shape[axis] for axis in ("gx", "gy", "gz"))
    return jax.shard_map(
        functools.partial(local, sizes),
        mesh=mesh,
        in_specs=(cells,) * 6 + (P(), P("rooms", None), P("rooms", None)),
        out_specs=(cells, cells, P("rooms")),
        check_vma=False,
    )
```
